256 devices in a mesh: rows: 64 (over z, y, core), cols: 4 (over x).
Axes of the slice: x: 4, y: 4, z: 8, core: 2. Of those that a mesh axis runs over, the one named last changes fastest.
Arguments:
- mutant_factors: bfloat16 [524288, 128], P(('rows', 'cols')), may hold values from -0.019334951 to 0.019334951
- test_factors: float32 [32768, 128], P('rows'), may hold values from -6 to 6
- weights: bfloat16 [64, 4, 28, 256, 256], P('rows', 'cols'), may hold values from 1 to 100
- pattern: int32 [64, 4, 28, 256, 256], P('rows', 'cols'), may hold values 0 or 1
- tile_block: int32 [64, 4, 28], P('rows', 'cols'), may hold values from 0 to 1
- hub_pick: int32 [64, 4, 8], P('rows', 'cols'), may hold values from 0 to 7
- hub_blocks: int32 [8], replicated, may hold values from 0 to 2047, as said below
- tail_req: int32 [64, 4, 64, 80], P('rows', 'cols'), may hold values from 0 to 2047
- tail_pick: int32 [64, 4, 5120], P('rows', 'cols'), may hold values from 0 to 5119, each once within a row
Outputs:
- test_solution: float32 [32768, 128], P(('rows', 'cols'))
- test_residual: float32 [32768, 128], P(('rows', 'cols'))
The draws below stay inside these ranges and needn't reach their ends.
Inputs may be any that keep to these rules, and one draw needn't show every extreme that they name: `hub_blocks`: the 8 hub blocks are distinct, and the last mutant block is always one of them. tail_req[r, c, o, j] is a row among the 2048 mutant rows of the device at rows index o and cols index c. `tail_pick`: each device's list is a permutation.
All inputs are finite; a program needn't handle non-finite values. No bound on the sum of `pattern` on one device may be relied on, other than what follows from the above.
Results may differ from the reference program's by a relative error of at most 0.003.
Values may be sent and summed in bfloat16 or wider, within the bound.
A program may use at most 128 MiB of HBM per device.

```python
import math
import jax
import jax.numpy as jnp
from jax import lax

K = 128
TILE = 256
ITERS = 2
HUB = 8
TB = 2
NH = 8
NL = 20
NT = 28
CAP = 80
MUT_DEV = 2048
MBLOCKS = 2048
MUTANTS = 524288
TESTS = 32768
N_ROWS = 64
N_COLS = 4


def draw_mutant_factors(key, part):
    base_key = jax.random.fold_in(key, 11)
    scale_key = jax.random.fold_in(key, 12)
    base_draw = jnp.clip(jax.random.normal(base_key, (MUTANTS, K), jnp.float32), -6.0, 6.0)
    column_scale = jnp.exp(jax.random.uniform(scale_key, (K,), jnp.float32, jnp.log(0.3), jnp.log(3.0)))
    row_rise = jnp.exp(jnp.log(3.0) * jnp.arange(MUTANTS, dtype=jnp.float32) / MUTANTS)
    values = base_draw * column_scale[None, :] * row_rise[:, None] * (0.25 / jnp.sqrt(jnp.float32(MUTANTS)))
    return values.astype(jnp.bfloat16)


def draw_hub_blocks(key, part):
    pick_key = jax.random.fold_in(key, 21)
    order_key = jax.random.fold_in(key, 22)
    others = jax.random.permutation(pick_key, MBLOCKS - 1)[:HUB - 1].astype(jnp.int32)
    chosen = jnp.concatenate([others, jnp.full((1,), MBLOCKS - 1, jnp.int32)])
    return jax.random.permutation(order_key, chosen).astype(jnp.int32)


def set_ends(entries, own_key, smallest, largest):
    place = [jax.random.randint(jax.random.fold_in(own_key, axis), (), 0, length) for axis, length in enumerate(entries.shape)]
    main_axis = entries.shape.index(max(entries.shape))
    beside = place[:main_axis] + [(place[main_axis] + 1) % entries.shape[main_axis]] + place[main_axis + 1:]
    return entries.at[tuple(place)].set(smallest).at[tuple(beside)].set(largest)


def block_scale(stream_key, extent, cuts, least, largest):
    level, own = 1.0, jax.random.fold_in(stream_key, 6)
    for position, parts in cuts:
        heights = jnp.exp(jax.random.uniform(jax.random.fold_in(own, position), (parts,), jnp.float32, least / len(cuts), largest / len(cuts)))
        level = level * jnp.repeat(heights, extent[position] // parts).reshape([-1 if axis == position else 1 for axis in range(len(extent))])
    return level


def centred(key, extent, deviation, bound, shards=(), kind=jnp.bfloat16):
    loudness = block_scale(key, extent, shards, -0.22, 0.18) if shards else 1.0
    drawn = jax.random.normal(key, extent, jnp.float32) * deviation * loudness
    return jnp.minimum(jnp.maximum(drawn, -bound), bound).astype(kind)


def setup_inputs(seed: int = 0) -> dict:
    seeds = jax.random.split(jax.random.key(seed), 10)
    mutant_factors = draw_mutant_factors(jax.random.fold_in(seeds[9], 71), 0)
    test_factors = centred(seeds[1], (TESTS, K), 1.0, 6.0, ((0, 64),), jnp.float32)
    weights = jnp.clip(jnp.exp(math.log(100.0) - 4.6051702 * jax.random.uniform(seeds[2], (N_ROWS, N_COLS, NT, TILE, TILE), jnp.float32) ** block_scale(seeds[2], (N_ROWS, N_COLS, NT, TILE, TILE), ((0, 64), (1, 4)), -0.2, 0.2)), 1.0, 100.0).astype(jnp.bfloat16)
    pattern = set_ends((jax.random.randint(seeds[3], (N_ROWS, N_COLS, NT, TILE, TILE), 0, 2) < 1).astype(jnp.int32), jax.random.fold_in(seeds[3], 1), 0, 1)
    tile_block = set_ends(jax.random.randint(seeds[4], (N_ROWS, N_COLS, NT), 0, TB), jax.random.fold_in(seeds[4], 1), 0, TB - 1).astype(jnp.int32)
    hub_pick = set_ends(jax.random.randint(seeds[5], (N_ROWS, N_COLS, NH), 0, HUB), jax.random.fold_in(seeds[5], 1), 0, HUB - 1).astype(jnp.int32)
    hub_blocks = draw_hub_blocks(jax.random.fold_in(seeds[9], 71), 0)
    tail_req = set_ends(jax.random.randint(seeds[7], (N_ROWS, N_COLS, N_ROWS, CAP), 0, MUT_DEV), jax.random.fold_in(seeds[7], 1), 0, MUT_DEV - 1).astype(jnp.int32)
    tail_pick = jax.vmap(lambda own: jax.random.permutation(own, NL * TILE))(jax.random.split(seeds[8], N_ROWS * N_COLS)).reshape((N_ROWS, N_COLS, NL * TILE)).astype(jnp.int32)
    return {"mutant_factors": mutant_factors, "test_factors": test_factors, "weights": weights, "pattern": pattern, "tile_block": tile_block, "hub_pick": hub_pick, "hub_blocks": hub_blocks, "tail_req": tail_req, "tail_pick": tail_pick}


ridge = 0.1
tiny = 1e-6
highest = lax.Precision.HIGHEST


def reference(mutant_factors, test_factors, weights, pattern, tile_block, hub_pick, hub_blocks, tail_req, tail_pick):
    gram_matrix = jnp.dot(mutant_factors.T, mutant_factors, preferred_element_type=jnp.float32)
    hub_rows = mutant_factors.reshape(MBLOCKS, TILE, K)[hub_blocks]
    owner_base = (jnp.arange(N_ROWS, dtype=jnp.int32)[None, None, :, None] * N_COLS
                  + jnp.arange(N_COLS, dtype=jnp.int32)[None, :, None, None]) * MUT_DEV
    global_ids = (owner_base + tail_req).reshape(N_ROWS, N_COLS, N_ROWS * CAP)
    picked_ids = jnp.take_along_axis(global_ids, tail_pick, axis=2).astype(jnp.int32)
    start_parts = test_factors.reshape(N_ROWS, TB * TILE, K)

    def partition(inputs):
        part_weights, part_pattern, part_blocks, part_hubs, part_ids, part_start = inputs
        hub_tiles = hub_rows[part_hubs]
        tail_tiles = mutant_factors[part_ids].reshape(N_COLS, NL, TILE, K)
        tile_factors = jnp.concatenate([hub_tiles, tail_tiles], axis=1).astype(jnp.float32)
        eff_weight = (part_weights * part_pattern.astype(jnp.bfloat16)).astype(jnp.float32)
        confidence = (part_pattern.astype(jnp.float32) * (1.0 + part_weights.astype(jnp.float32))).astype(jnp.bfloat16)
        confidence = lax.optimization_barrier(confidence).astype(jnp.float32)
        block_select = (part_blocks[..., None] == jnp.arange(TB, dtype=jnp.int32)).astype(jnp.float32)

        def spread(per_tile):
            return jnp.einsum("cnb,cntk->btk", block_select, per_tile, precision=highest).reshape(TB * TILE, K)

        def tile_product(vector):
            rounded = lax.optimization_barrier(vector.astype(jnp.bfloat16)).astype(jnp.float32)
            pieces = jnp.einsum("cnb,btk->cntk", block_select, rounded.reshape(TB, TILE, K), precision=highest)
            scores = jnp.einsum("cntk,cnmk->cntm", pieces, tile_factors, precision=highest)
            weighted = lax.optimization_barrier((scores * eff_weight).astype(jnp.bfloat16)).astype(jnp.float32)
            return spread(jnp.einsum("cntm,cnmk->cntk", weighted, tile_factors, precision=highest))

        def apply_operator(vector):
            return tile_product(vector) + jnp.dot(vector, gram_matrix, precision=highest) + ridge * vector

        right_side = spread(jnp.einsum("cntm,cnmk->cntk", confidence, tile_factors, precision=highest))
        solution = part_start
        residual = right_side - apply_operator(solution)
        direction = residual
        norm_now = jnp.sum(residual * residual, axis=1, keepdims=True)
        for iteration in range(ITERS):
            applied = apply_operator(direction)
            step_size = norm_now / (jnp.sum(direction * applied, axis=1, keepdims=True) + tiny)
            solution = solution + step_size * direction
            residual = residual - step_size * applied
            norm_next = jnp.sum(residual * residual, axis=1, keepdims=True)
            direction = residual + (norm_next / (norm_now + tiny)) * direction
            norm_now = norm_next
        return solution, residual

    solutions, residuals = lax.map(partition, (weights, pattern, tile_block, hub_pick, picked_ids, start_parts))
    return solutions.reshape(TESTS, K), residuals.reshape(TESTS, K)
```

```python
import functools

import jax
import jax.numpy as jnp
from jax import lax
from jax.experimental import pallas as pl
from jax.experimental.pallas import tpu as pltpu
from jax.sharding import PartitionSpec as P

ITERS = 2

ridge = 0.1
tiny = 1e-06
highest = lax.Precision.HIGHEST
f32 = jnp.float32
bf16 = jnp.bfloat16


def fold(a, b):
    return lax.dot_general(a, b, (((0,), (0,)), ((), ())), preferred_element_type=f32)


def across(a, b):
    return lax.dot_general(a, b, (((1,), (1,)), ((), ())), preferred_element_type=f32)


def plain(a, b):
    return jnp.dot(a, b, preferred_element_type=f32)


def remote(src, dst, send_sem, recv_sem, row, col):
    return pltpu.make_async_remote_copy(
        src_ref=src,
        dst_ref=dst,
        send_sem=send_sem,
        recv_sem=recv_sem,
        device_id=(row, col),
        device_id_type=pl.DeviceIdType.MESH,
    )


def drain(ref, sem):
    pltpu.make_async_copy(ref, ref, sem).wait()


def kernel(
    dims,
    mutants_h,
    start_h,
    weights_h,
    pattern_h,
    requests_h,
    pick_h,
    block_s,
    hub_pick_s,
    hub_block_s,
    solution_ref,
    residual_ref,
    mutants,
    mutants32,
    start,
    weights,
    pattern,
    confidence,
    requests,
    pick_s,
    asked_out,
    asked_in,
    asked_s,
    rows32,
    answers,
    received,
    tail32,
    tile32,
    tail,
    hub_mine,
    hub_x,
    hub_xsum,
    hub_y,
    hub_ysum,
    hub_z,
    hub_share,
    hub_all,
    gram_mine,
    gram_x,
    gram_xsum,
    gram_y,
    gram_ysum,
    gram_z,
    gram_zsum,
    gram_all,
    start_half,
    direction_half,
    terms,
    terms_in,
    local_sem,
    asked_sem,
    answer_send,
    answer_recv,
    hub_send,
    hub_recv,
    gram_send,
    gram_recv,
    terms_send,
    terms_recv,
    dir_send,
    dir_recv,
):
    n_rows, n_cols, planes, ring, cap, tile, tiles, hub_tiles, hubs = dims
    row = lax.axis_index("rows")
    col = lax.axis_index("cols")
    z = lax.div(row, ring)
    yc = lax.rem(row, ring)
    tail_tiles = tiles - hub_tiles

    def near_x(k):
        return lax.rem(col + k, n_cols)

    def near_y(k):
        return lax.rem(yc + k, ring)

    def near_z(k):
        return lax.rem(z + k, planes)

    def partner(i):
        k = lax.rem(i, planes)
        half = lax.div(k + 1, 2)
        dz = planes // 2 + half * (1 - 2 * lax.rem(k, 2))
        dy = lax.div(i, planes) + 1
        return lax.rem(z + dz, planes) * ring + lax.rem(yc + dy, ring)

    dir_words = (n_cols - 1) * (start.shape[0] // n_cols) // hub_ysum.shape[0]

    local = [
        pltpu.make_async_copy(requests_h, requests, local_sem.at[0]),
        pltpu.make_async_copy(mutants_h, mutants, local_sem.at[1]),
        pltpu.make_async_copy(pick_h, pick_s, local_sem.at[2]),
        pltpu.make_async_copy(start_h, start, local_sem.at[3]),
        pltpu.make_async_copy(weights_h, weights, local_sem.at[4]),
        pltpu.make_async_copy(pattern_h, pattern, local_sem.at[5]),
    ]
    for copy in local:
        copy.start()

    barrier = pltpu.get_barrier_semaphore()

    def greet(i, carry):
        pl.semaphore_signal(
            barrier, inc=1, device_id=(partner(i), col), device_id_type=pl.DeviceIdType.MESH
        )
        return carry

    lax.fori_loop(0, n_rows - 1, greet, 0)
    for k in range(1, n_cols):
        pl.semaphore_signal(
            barrier, inc=1, device_id=(row, near_x(k)), device_id_type=pl.DeviceIdType.MESH
        )
    local[0].wait()
    for o in range(n_rows):
        asked_out[o, :, 0:cap] = requests[o : o + 1, :]
    pl.semaphore_wait(barrier, n_rows + n_cols - 2)

    def ask(i, carry):
        d = partner(i)
        remote(asked_out.at[d], asked_in.at[row], asked_sem.at[0], asked_sem.at[1], d, col).start()
        return carry

    lax.fori_loop(0, n_rows - 1, ask, 0)
    asked_in[row] = asked_out[row]

    local[1].wait()
    rows_here = mutants[...].reshape(mutants32.shape)
    gram = fold(rows_here, rows_here)
    share = gram.shape[0] // n_cols
    for q in range(n_cols):
        gram_mine[q] = gram[q * share : (q + 1) * share]
    blocks_here = mutants.shape[0]
    me = row * n_cols + col
    for h in range(hubs):
        block = hub_block_s[h]
        own = mutants[lax.rem(block, blocks_here)]
        owner = jnp.full(own.shape, lax.div(block, blocks_here), jnp.int32)
        hub_mine[h] = jnp.where(owner == me, own.astype(f32), 0.0).astype(bf16)
    per_col = hubs // n_cols
    for k in (2, 1, 3):
        q = near_x(k)
        remote(
            hub_mine.at[pl.ds(q * per_col, per_col)], hub_x.at[col],
            hub_send.at[0], hub_recv.at[0], row, q,
        ).start()
        remote(
            gram_mine.at[q], gram_x.at[col], gram_send.at[0], gram_recv.at[0], row, q
        ).start()
    for o in range(blocks_here):
        mutants32[o * tile : (o + 1) * tile] = mutants[o].astype(f32)

    drain(asked_in.at[pl.ds(0, n_rows - 1)], asked_sem.at[1])
    fetch = pltpu.make_async_copy(asked_in, asked_s, local_sem.at[6])
    fetch.start()
    fetch.wait()

    def gather_for(d):
        for j in range(cap):
            rows32[j : j + 1, :] = mutants32[pl.ds(asked_s[d, 0, j], 1), :]
        return rows32[...].astype(bf16)

    def serve(i, carry):
        d = partner(i)
        answers[i] = gather_for(d)
        remote(
            answers.at[i], received.at[row], answer_send, answer_recv.at[row], d, col
        ).start()
        return carry

    def prepare(n, carry):
        w = weights[n].astype(f32)
        p = pattern[n].astype(f32)
        weights[n] = (w * p).astype(bf16)
        confidence[n] = (p * (1.0 + w)).astype(bf16)
        return carry

    others = n_rows - 1
    cuts = [others * s // 5 for s in range(6)]

    lax.fori_loop(cuts[0], cuts[1], serve, 0)
    drain(hub_x.at[pl.ds(0, n_cols - 1)], hub_recv.at[0])
    drain(gram_x.at[pl.ds(0, n_cols - 1)], gram_recv.at[0])
    piece = hub_xsum.shape[1]
    total = hub_mine[pl.ds(col * per_col, per_col)]
    for k in range(1, n_cols):
        total = total + hub_x[near_x(k)]
    hub_xsum[...] = total.reshape(hub_xsum.shape)
    gsum = gram_mine[col]
    for k in range(1, n_cols):
        gsum = gsum + gram_x[near_x(k)]
    gram_xsum[...] = gsum
    for k in range(1, ring):
        e = near_y(k)
        remote(
            hub_xsum.at[e], hub_y.at[yc], hub_send.at[1], hub_recv.at[1], z * ring + e, col
        ).start()
        remote(
            gram_xsum, gram_y.at[yc], gram_send.at[1], gram_recv.at[1], z * ring + e, col
        ).start()

    lax.fori_loop(cuts[1], cuts[2], serve, 0)
    drain(hub_y.at[pl.ds(0, ring - 1)], hub_recv.at[1])
    drain(gram_y.at[pl.ds(0, ring - 1)], gram_recv.at[1])
    total = hub_xsum[yc]
    gsum = gram_xsum[...]
    for k in range(1, ring):
        total = total + hub_y[near_y(k)]
        gsum = gsum + gram_y[near_y(k)]
    hub_ysum[...] = total
    gram_ysum[...] = gsum
    for k in range(1, planes):
        e = near_z(k)
        remote(
            hub_ysum, hub_z.at[z], hub_send.at[2], hub_recv.at[2], e * ring + yc, col
        ).start()
        remote(
            gram_ysum, gram_z.at[z], gram_send.at[2], gram_recv.at[2], e * ring + yc, col
        ).start()

    lax.fori_loop(cuts[2], cuts[3], serve, 0)
    drain(hub_z.at[pl.ds(0, planes - 1)], hub_recv.at[2])
    drain(gram_z.at[pl.ds(0, planes - 1)], gram_recv.at[2])
    total = hub_ysum[...]
    gsum = gram_ysum[...]
    for k in range(1, planes):
        total = total + hub_z[near_z(k)]
        gsum = gsum + gram_z[near_z(k)]
    pieces = ring // per_col
    my_piece = hub_share.at[lax.div(yc, pieces), lax.rem(yc, pieces)]
    my_piece[...] = total
    gram_zsum[...] = gsum
    for k in range(1, ring):
        e = near_y(k)
        remote(
            my_piece, my_piece, hub_send.at[3], hub_recv.at[3], z * ring + e, col
        ).start()
    for k in range(1, n_cols):
        remote(
            gram_zsum, gram_all.at[col], gram_send.at[3], gram_recv.at[3], row, near_x(k)
        ).start()
    gram_all[col] = gsum

    lax.fori_loop(cuts[3], cuts[4], serve, 0)
    drain(hub_y.at[pl.ds(0, ring - 1)], hub_recv.at[3])
    my_hubs = pl.ds(col * per_col, per_col)
    for k in range(1, n_cols):
        remote(
            hub_share, hub_all.at[my_hubs], hub_send.at[4], hub_recv.at[4], row, near_x(k)
        ).start()
    lax.fori_loop(cuts[4], cuts[5], serve, 0)
    received[row] = gather_for(row)
    hub_all[my_hubs] = hub_share[...]
    local[4].wait()
    local[5].wait()
    lax.fori_loop(0, tiles, prepare, 0)
    local[3].wait()
    quarter = start.shape[0] // n_cols
    block_quarters = tile // quarter
    for q in range(n_cols):
        start_half[q // block_quarters, q % block_quarters] = start[q * quarter : (q + 1) * quarter].astype(bf16)
    drain(hub_all.at[pl.ds(0, hubs - per_col)], hub_recv.at[4])
    drain(gram_all.at[pl.ds(0, n_cols - 1)], gram_recv.at[3])


    def hub_tile(n):
        part = hub_all[hub_pick_s[n]]
        return part.reshape(tile, part.shape[-1])

    def add_up(step, block, product):
        parts = product.reshape(block_quarters, quarter, product.shape[-1])
        covers = jnp.full(parts.shape, block, jnp.int32)
        for b in range(2):
            at = slice(b * block_quarters, (b + 1) * block_quarters)
            terms[step, at] += jnp.where(covers == b, parts, 0.0)

    def scores_of(vector, n, factors):
        b = block_s[n]
        v = vector[b].reshape(tile, factors.shape[-1])
        weighted = (across(v, factors) * weights[n].astype(f32)).astype(bf16)
        return b, weighted

    def first(n, factors):
        b, weighted = scores_of(start_half, n, factors)
        add_up(0, b, plain(confidence[n], factors) - plain(weighted, factors))

    def later(step, n, factors):
        b, weighted = scores_of(direction_half.at[step - 1], n, factors)
        add_up(step, b, plain(weighted, factors))

    for step in range(ITERS + 1):
        terms[step] = jnp.zeros(terms.shape[1:], f32)

    def hub_first(n, carry):
        first(n, hub_tile(n))
        return carry

    lax.fori_loop(0, hub_tiles, hub_first, 0)

    def arrive(i, carry):
        o = partner(i)
        remote(
            answers.at[i], received.at[o], answer_send, answer_recv.at[o], o, col
        ).wait_recv()
        tail32[pl.ds(pl.multiple_of(o * cap, cap), cap), :] = received[o].astype(f32)
        return carry

    lax.fori_loop(0, others, arrive, 0)
    tail32[pl.ds(pl.multiple_of(row * cap, cap), cap), :] = received[row].astype(f32)

    def tail_first(l, carry):
        for i in range(tile):
            tile32[i : i + 1, :] = tail32[pl.ds(pick_s[l * tile + i], 1), :]
        factors = tile32[...].astype(bf16)
        tail[l] = factors
        first(l + hub_tiles, factors)
        return carry

    local[2].wait()
    lax.fori_loop(0, tail_tiles, tail_first, 0)

    def reduce_terms(step):
        for k in (2, 1, 3):
            q = near_x(k)
            remote(
                terms.at[step, q], terms_in.at[step, col],
                terms_send.at[step], terms_recv.at[step], row, q,
            ).start()
        drain(terms_in.at[step, pl.ds(0, n_cols - 1)], terms_recv.at[step])
        total = terms[step, col]
        for k in range(1, n_cols):
            total = total + terms_in[step, near_x(k)]
        return total

    gram_matrix = gram_all[...].reshape(gram.shape)

    def operator_rest(vector):
        return (
            jnp.dot(vector, gram_matrix, precision=highest, preferred_element_type=f32)
            + ridge * vector
        )

    solution = start[pl.ds(pl.multiple_of(col * quarter, quarter), quarter), :]
    residual = reduce_terms(0) - operator_rest(solution)
    direction = residual
    norm_now = jnp.sum(residual * residual, axis=1, keepdims=True)
    for iteration in range(ITERS):
        mine = direction_half.at[
            iteration, lax.div(col, block_quarters), lax.rem(col, block_quarters)
        ]
        mine[...] = direction.astype(bf16)
        for k in (2, 1, 3):
            remote(
                mine, mine, dir_send.at[iteration], dir_recv.at[iteration], row, near_x(k)
            ).start()
        rest = operator_rest(direction)
        drain(hub_xsum.at[pl.ds(0, dir_words)], dir_recv.at[iteration])

        def hub_later(n, carry):
            later(iteration + 1, n, hub_tile(n))
            return carry

        def tail_later(l, carry):
            later(iteration + 1, l + hub_tiles, tail[l])
            return carry

        lax.fori_loop(0, hub_tiles, hub_later, 0)
        lax.fori_loop(0, tail_tiles, tail_later, 0)
        applied = reduce_terms(iteration + 1) + rest
        step_size = norm_now / (jnp.sum(direction * applied, axis=1, keepdims=True) + tiny)
        solution = solution + step_size * direction
        residual = residual - step_size * applied
        norm_next = jnp.sum(residual * residual, axis=1, keepdims=True)
        direction = residual + norm_next / (norm_now + tiny) * direction
        norm_now = norm_next
    solution_ref[...] = solution
    residual_ref[...] = residual

    drain(asked_out.at[pl.ds(0, n_rows - 1)], asked_sem.at[0])
    drain(answers.at[pl.ds(0, n_rows - 1)], answer_send)
    drain(hub_x.at[pl.ds(0, n_cols - 1)], hub_send.at[0])
    drain(hub_y.at[pl.ds(0, ring - 1)], hub_send.at[1])
    drain(hub_z.at[pl.ds(0, planes - 1)], hub_send.at[2])
    drain(hub_y.at[pl.ds(0, ring - 1)], hub_send.at[3])
    drain(hub_all.at[pl.ds(0, hubs - per_col)], hub_send.at[4])
    drain(gram_x.at[pl.ds(0, n_cols - 1)], gram_send.at[0])
    drain(gram_y.at[pl.ds(0, ring - 1)], gram_send.at[1])
    drain(gram_z.at[pl.ds(0, planes - 1)], gram_send.at[2])
    drain(gram_all.at[pl.ds(0, n_cols - 1)], gram_send.at[3])
    for step in range(ITERS + 1):
        drain(terms_in.at[step, pl.ds(0, n_cols - 1)], terms_send.at[step])
    for iteration in range(ITERS):
        drain(hub_xsum.at[pl.ds(0, dir_words)], dir_send.at[iteration])


def per_device(
    n_rows,
    n_cols,
    mutant_factors,
    test_factors,
    weights,
    pattern,
    tile_block,
    hub_pick,
    hub_blocks,
    tail_req,
    tail_pick,
):
    mutant_rows, width = mutant_factors.shape
    tile = weights.shape[-1]
    tiles = weights.shape[2]
    hub_tiles = hub_pick.shape[2]
    hubs = hub_blocks.shape[0]
    cap = tail_req.shape[-1]
    full_rows = test_factors.shape[0]
    share = full_rows // n_cols
    slots = (tiles - hub_tiles) * tile
    ring = 8 if n_rows % 64 == 0 else 2
    planes = n_rows // ring
    per_col = hubs // n_cols
    piece = per_col * tile // ring
    gram_share = width // n_cols
    dims = (n_rows, n_cols, planes, ring, cap, tile, tiles, hub_tiles, hubs)
    vmem = pltpu.VMEM
    dma = pltpu.SemaphoreType.DMA
    scratch = [
        vmem((mutant_rows // tile, tile, width), bf16),
        vmem((mutant_rows, width), f32),
        vmem((full_rows, width), f32),
        vmem((tiles, tile, tile), bf16),
        vmem((tiles, tile, tile), jnp.int32),
        vmem((tiles, tile, tile), bf16),
        vmem((n_rows, cap), jnp.int32),
        pltpu.SMEM((slots,), jnp.int32),
        vmem((n_rows, 1, 128), jnp.int32),
        vmem((n_rows, 1, 128), jnp.int32),
        pltpu.SMEM((n_rows, 1, 128), jnp.int32),
        vmem((cap, width), f32),
        vmem((n_rows, cap, width), bf16),
        vmem((n_rows, cap, width), bf16),
        vmem((slots, width), f32),
        vmem((tile, width), f32),
        vmem((tiles - hub_tiles, tile, width), bf16),
        vmem((hubs, tile, width), bf16),
        vmem((n_cols, per_col, tile, width), bf16),
        vmem((ring, piece, width), bf16),
        vmem((ring, piece, width), bf16),
        vmem((piece, width), bf16),
        vmem((planes, piece, width), bf16),
        vmem((per_col, ring // per_col, piece, width), bf16),
        vmem((hubs, ring // per_col, piece, width), bf16),
        vmem((n_cols, gram_share, width), f32),
        vmem((n_cols, gram_share, width), f32),
        vmem((gram_share, width), f32),
        vmem((ring, gram_share, width), f32),
        vmem((gram_share, width), f32),
        vmem((planes, gram_share, width), f32),
        vmem((gram_share, width), f32),
        vmem((n_cols, gram_share, width), f32),
        vmem((2, n_cols // 2, share, width), bf16),
        vmem((ITERS, 2, n_cols // 2, share, width), bf16),
        vmem((ITERS + 1, n_cols, share, width), f32),
        vmem((ITERS + 1, n_cols, share, width), f32),
        dma((7,)),
        dma((2,)),
        dma,
        dma((n_rows,)),
        dma((5,)),
        dma((5,)),
        dma((4,)),
        dma((4,)),
        dma((ITERS + 1,)),
        dma((ITERS + 1,)),
        dma((ITERS,)),
        dma((ITERS,)),
    ]
    anywhere = pl.BlockSpec(memory_space=pl.ANY)
    scalars = pl.BlockSpec(memory_space=pltpu.SMEM)
    out = jax.ShapeDtypeStruct((share, width), f32)
    return pl.pallas_call(
        functools.partial(kernel, dims),
        out_shape=(out, out),
        in_specs=[anywhere] * 6 + [scalars] * 3,
        out_specs=(pl.BlockSpec(memory_space=vmem),) * 2,
        scratch_shapes=scratch,
        compiler_params=pltpu.CompilerParams(
            collective_id=0, has_side_effects=True, vmem_limit_bytes=56 * 1024 * 1024
        ),
    )(
        mutant_factors.reshape(-1, tile, width),
        test_factors,
        weights.reshape(weights.shape[2:]),
        pattern.reshape(pattern.shape[2:]),
        tail_req.reshape(tail_req.shape[2:]),
        tail_pick.reshape(slots),
        tile_block.reshape(tiles),
        hub_pick.reshape(hub_tiles),
        hub_blocks,
    )


def solution(mesh):
    in_specs = (
        P(("rows", "cols"), None),
        P("rows", None),
        P("rows", "cols", None, None, None),
        P("rows", "cols", None, None, None),
        P("rows", "cols", None),
        P("rows", "cols", None),
        P(),
        P("rows", "cols", None, None),
        P("rows", "cols", None),
    )
    out_specs = (P(("rows", "cols"), None), P(("rows", "cols"), None))
    return jax.shard_map(
        functools.partial(per_device, mesh.shape["rows"], mesh.shape["cols"]),
        mesh=mesh,
        in_specs=in_specs,
        out_specs=out_specs,
        check_vma=False,
    )
```

```python
import functools

import jax
import jax.numpy as jnp
from jax import lax
from jax.experimental import pallas as pl
from jax.experimental.pallas import tpu as pltpu
from jax.sharding import PartitionSpec as P

ITERS = 2
GROUP = 4

ridge = 0.1
tiny = 1e-06
highest = lax.Precision.HIGHEST
f32 = jnp.float32
bf16 = jnp.bfloat16


def fold(a, b):
    return lax.dot_general(a, b, (((0,), (0,)), ((), ())), preferred_element_type=f32)


def across(a, b):
    return lax.dot_general(a, b, (((1,), (1,)), ((), ())), preferred_element_type=f32)


def plain(a, b):
    return jnp.dot(a, b, preferred_element_type=f32)


def remote(src, dst, send_sem, recv_sem, row, col):
    return pltpu.make_async_remote_copy(
        src_ref=src,
        dst_ref=dst,
        send_sem=send_sem,
        recv_sem=recv_sem,
        device_id=(row, col),
        device_id_type=pl.DeviceIdType.MESH,
    )


def drain(ref, sem):
    pltpu.make_async_copy(ref, ref, sem).wait()


def kernel(
    dims,
    mutants_h,
    start_h,
    weights_h,
    pattern_h,
    requests_h,
    pick_h,
    block_s,
    hub_pick_s,
    hub_block_s,
    out_ref,
    mutants,
    mutants32,
    start,
    weights,
    pattern,
    confidence,
    requests,
    pick_s,
    asked_out,
    asked_in,
    asked_s,
    rows32,
    answers,
    received,
    tail32,
    tile32,
    factors,
    hub_mine,
    hub_x,
    hub_xsum,
    hub_y,
    hub_ysum,
    hub_z,
    hub_share,
    hub_all,
    gram_mine,
    gram_x,
    gram_xsum,
    gram_y,
    gram_ysum,
    gram_z,
    gram_all,
    start_half,
    direction_half,
    terms,
    terms_in,
    local_sem,
    asked_sem,
    answer_send,
    answer_recv,
    hub_send,
    hub_recv,
    gram_send,
    gram_recv,
    terms_send,
    terms_recv,
    dir_send,
    dir_recv,
):
    n_rows, n_cols, planes, ring, cap, tile, tiles, hub_tiles, hubs = dims
    row = lax.axis_index("rows")
    col = lax.axis_index("cols")
    z = lax.div(row, ring)
    yc = lax.rem(row, ring)
    tail_tiles = tiles - hub_tiles

    def near_x(k):
        return lax.rem(col + k, n_cols)

    def near_y(k):
        return lax.rem(yc + k, ring)

    def near_z(k):
        return lax.rem(z + k, planes)

    def partner(i):
        k = lax.rem(i, planes)
        half = lax.div(k + 1, 2)
        dz = planes // 2 + half * (1 - 2 * lax.rem(k, 2))
        dy = lax.div(i, planes) + 1
        return lax.rem(z + dz, planes) * ring + lax.rem(yc + dy, ring)

    dir_words = (n_cols - 1) * (start.shape[0] // n_cols) // hub_ysum.shape[0]

    local = [
        pltpu.make_async_copy(requests_h, requests, local_sem.at[0]),
        pltpu.make_async_copy(mutants_h, mutants, local_sem.at[1]),
        pltpu.make_async_copy(pick_h, pick_s, local_sem.at[2]),
        pltpu.make_async_copy(start_h, start, local_sem.at[3]),
        pltpu.make_async_copy(weights_h, weights, local_sem.at[4]),
        pltpu.make_async_copy(pattern_h, pattern, local_sem.at[5]),
    ]
    for copy in local:
        copy.start()

    barrier = pltpu.get_barrier_semaphore()

    def greet(i, carry):
        pl.semaphore_signal(
            barrier, inc=1, device_id=(partner(i), col), device_id_type=pl.DeviceIdType.MESH
        )
        return carry

    lax.fori_loop(0, n_rows - 1, greet, 0)
    for k in range(1, n_cols):
        pl.semaphore_signal(
            barrier, inc=1, device_id=(row, near_x(k)), device_id_type=pl.DeviceIdType.MESH
        )
    local[0].wait()
    for o in range(n_rows):
        asked_out[o, :, 0:cap] = requests[o : o + 1, :]
    pl.semaphore_wait(barrier, n_rows + n_cols - 2)

    def ask(i, carry):
        d = partner(i)
        remote(asked_out.at[d], asked_in.at[row], asked_sem.at[0], asked_sem.at[1], d, col).start()
        return carry

    lax.fori_loop(0, n_rows - 1, ask, 0)
    asked_in[row] = asked_out[row]

    local[1].wait()
    blocks_here = mutants.shape[0]
    for o in range(blocks_here):
        mutants32[o * tile : (o + 1) * tile] = mutants[o].astype(f32)
    me = row * n_cols + col
    per_col = hubs // n_cols
    pieces = ring // per_col
    for h in range(hubs):
        block = hub_block_s[h]
        own = mutants[lax.rem(block, blocks_here)]
        owner = jnp.full(own.shape, lax.div(block, blocks_here), jnp.int32)
        kept = jnp.where(owner == me, own.astype(f32), 0.0).astype(bf16)
        at = slice(h % per_col * pieces, (h % per_col + 1) * pieces)
        hub_mine[h // per_col, at] = kept.reshape(pieces, tile // pieces, kept.shape[-1])

    def send_hub_x(p):
        q = near_x(lax.rem(p, n_cols - 1) + 1)
        e = lax.div(p, n_cols - 1)
        remote(
            hub_mine.at[q, e], hub_x.at[col, e], hub_send.at[0], hub_recv.at[0], row, q
        ).start()

    hub_pieces = (n_cols - 1) * ring
    early = hub_pieces // 3
    for p in range(early):
        send_hub_x(p)

    drain(asked_in.at[pl.ds(0, n_rows - 1)], asked_sem.at[1])
    fetch = pltpu.make_async_copy(asked_in, asked_s, local_sem.at[6])
    fetch.start()
    fetch.wait()

    def gather_for(d):
        for j in range(cap):
            rows32[j : j + 1, :] = mutants32[pl.ds(asked_s[d, 0, j], 1), :]
        return rows32[...].astype(bf16)

    def serve(i, carry):
        d = partner(i)
        answers[i] = gather_for(d)
        remote(
            answers.at[i], received.at[row], answer_send, answer_recv.at[row], d, col
        ).start()
        return carry

    def prepare(n, carry):
        w = weights[n].astype(f32)
        p = pattern[n].astype(f32)
        weights[n] = (w * p).astype(bf16)
        confidence[n] = (p * (1.0 + w)).astype(bf16)
        return carry

    others = n_rows - 1
    def serve_and_send(i, carry):
        serve(i, carry)
        send_hub_x(early + i)
        return carry

    def serve_and_send(i, carry):
        serve(i, carry)
        send_hub_x(early + i)
        return carry

    cuts = [hub_pieces - early, others * 4 // 9, others * 2 // 3]
    ready = [tiles * c // 4 for c in range(5)]

    first_cut = hub_pieces - early
    cuts = [first_cut] + [first_cut + (others - first_cut) * c // 47 for c in (12, 26)]
    ready = [tiles * c // 3 for c in range(4)]

    lax.fori_loop(0, cuts[0], serve_and_send, 0)
    rows_here = mutants[...].reshape(mutants32.shape)
    gram = fold(rows_here, rows_here)
    share = gram_mine.shape[1]
    for q in range(ring):
        gram_mine[q] = gram[q * share : (q + 1) * share]
    for k in range(1, ring):
        e = near_y(k)
        remote(
            gram_mine.at[e], gram_y.at[yc], gram_send.at[0], gram_recv.at[0], z * ring + e, col
        ).start()
    lax.fori_loop(cuts[0], cuts[1], serve, 0)
    local[4].wait()
    local[5].wait()
    lax.fori_loop(ready[0], ready[1], prepare, 0)

    drain(hub_x.at[pl.ds(0, n_cols - 1)], hub_recv.at[0])
    total = hub_mine[col]
    for k in range(1, n_cols):
        total = total + hub_x[near_x(k)]
    hub_xsum[...] = total
    for k in range(1, ring):
        e = near_y(k)
        remote(
            hub_xsum.at[e], hub_y.at[yc], hub_send.at[1], hub_recv.at[1], z * ring + e, col
        ).start()
    drain(gram_y.at[pl.ds(0, ring - 1)], gram_recv.at[0])
    gsum = gram_mine[yc]
    for k in range(1, ring):
        gsum = gsum + gram_y[near_y(k)]
    gram_ysum[...] = gsum
    for k in range(1, n_cols):
        remote(
            gram_ysum, gram_x.at[col], gram_send.at[1], gram_recv.at[1], row, near_x(k)
        ).start()
    lax.fori_loop(cuts[1], cuts[2], serve, 0)
    lax.fori_loop(ready[1], ready[2], prepare, 0)

    drain(hub_y.at[pl.ds(0, ring - 1)], hub_recv.at[1])
    total = hub_xsum[yc]
    for k in range(1, ring):
        total = total + hub_y[near_y(k)]
    hub_ysum[...] = total
    for k in range(1, planes):
        e = near_z(k)
        remote(
            hub_ysum, hub_z.at[z], hub_send.at[2], hub_recv.at[2], e * ring + yc, col
        ).start()
    drain(gram_x.at[pl.ds(0, n_cols - 1)], gram_recv.at[1])
    gsum = gram_ysum[...]
    for k in range(1, n_cols):
        gsum = gsum + gram_x[near_x(k)]
    gram_xsum[...] = gsum
    lax.fori_loop(cuts[2], others, serve, 0)
    for k in range(1, planes):
        e = near_z(k)
        remote(
            gram_xsum, gram_z.at[z], gram_send.at[2], gram_recv.at[2], e * ring + yc, col
        ).start()
    lax.fori_loop(ready[2], ready[3], prepare, 0)
    received[row] = gather_for(row)
    local[3].wait()
    quarter = start.shape[0] // n_cols
    block_quarters = tile // quarter
    for q in range(n_cols):
        start_half[q // block_quarters, q % block_quarters] = start[
            q * quarter : (q + 1) * quarter
        ].astype(bf16)
    for step in range(ITERS + 1):
        terms[step] = jnp.zeros(terms.shape[1:], f32)

    def group(step, vector, base):
        parts = []
        for u in range(GROUP):
            n = base + u
            b = block_s[n]
            v = vector[b].reshape(tile, factors.shape[-1])
            scores = across(v, factors[n])
            parts.append((n, b, (scores * weights[n].astype(f32)).astype(bf16)))
        sums = [None, None]
        for n, b, weighted in parts:
            product = plain(weighted, factors[n])
            if step == 0:
                product = plain(confidence[n], factors[n]) - product
            covers = jnp.full(product.shape, b, jnp.int32)
            for half in range(2):
                kept = jnp.where(covers == half, product, 0.0)
                sums[half] = kept if sums[half] is None else sums[half] + kept
        for half in range(2):
            at = slice(half * block_quarters, (half + 1) * block_quarters)
            terms[step, at] += sums[half].reshape(block_quarters, quarter, factors.shape[-1])

    def groups(step, vector, first, last):
        def one(g, carry):
            group(step, vector, g * GROUP)
            return carry

        lax.fori_loop(first // GROUP, last // GROUP, one, 0)

    def arrive(i, carry):
        o = partner(i)
        remote(
            answers.at[i], received.at[o], answer_send, answer_recv.at[o], o, col
        ).wait_recv()
        tail32[pl.ds(pl.multiple_of(o * cap, cap), cap), :] = received[o].astype(f32)
        return carry

    lax.fori_loop(0, cuts[2], arrive, 0)

    drain(hub_z.at[pl.ds(0, planes - 1)], hub_recv.at[2])
    total = hub_ysum[...]
    for k in range(1, planes):
        total = total + hub_z[near_z(k)]
    core = lax.rem(yc, 2)
    my_piece = hub_share.at[lax.div(yc, pieces), lax.div(lax.rem(yc, pieces), 2)]
    my_piece[...] = total
    for k in range(2, ring, 2):
        remote(
            my_piece, my_piece, hub_send.at[3], hub_recv.at[3], z * ring + near_y(k), col
        ).start()
    lax.fori_loop(cuts[2], others, arrive, 0)
    tail32[pl.ds(pl.multiple_of(row * cap, cap), cap), :] = received[row].astype(f32)

    def tail_tile(l, carry):
        for i in range(tile):
            tile32[i : i + 1, :] = tail32[pl.ds(pick_s[l * tile + i], 1), :]
        factors[l + hub_tiles] = tile32[...].astype(bf16)
        return carry

    local[2].wait()

    drain(hub_y.at[pl.ds(0, ring // 2 - 1)], hub_recv.at[3])
    halves = pieces // 2
    for h in range(per_col):
        at = col * per_col + h
        for k in (2, 1, 3):
            remote(
                hub_share.at[h], hub_all.at[at, core],
                hub_send.at[4], hub_recv.at[4], row, near_x(k),
            ).start()
        hub_all[at, core] = hub_share[h]

    drain(gram_z.at[pl.ds(0, planes - 1)], gram_recv.at[2])
    gsum = gram_xsum[...]
    for k in range(1, planes):
        gsum = gsum + gram_z[near_z(k)]
    gram_all[yc] = gsum
    for k in range(1, ring):
        remote(
            gram_all.at[yc], gram_all.at[yc], gram_send.at[3], gram_recv.at[3],
            z * ring + near_y(k), col,
        ).start()
    middle = tail_tiles * 3 // 4
    lax.fori_loop(0, middle, tail_tile, 0)

    drain(hub_x.at[pl.ds(0, n_cols - 1), pl.ds(0, per_col * halves)], hub_recv.at[4])
    sibling = row + 1 - 2 * core
    for h in range(hubs):
        remote(
            hub_all.at[h, core], hub_all.at[h, core],
            hub_send.at[5], hub_recv.at[5], sibling, col,
        ).start()
    lax.fori_loop(middle, tail_tiles, tail_tile, 0)
    groups(0, start_half, hub_tiles, tiles)
    drain(hub_mine.at[pl.ds(0, n_cols // 2)], hub_recv.at[5])
    for n in range(hub_tiles):
        part = hub_all[hub_pick_s[n]]
        for m in range(halves):
            for c in range(2):
                at = (2 * m + c) * part.shape[2]
                factors[n, at : at + part.shape[2]] = part[c, m]
    groups(0, start_half, 0, hub_tiles)

    def reduce_terms(step):
        for k in (2, 1, 3):
            q = near_x(k)
            remote(
                terms.at[step, q], terms_in.at[step, col],
                terms_send.at[step], terms_recv.at[step], row, q,
            ).start()
        drain(terms_in.at[step, pl.ds(0, n_cols - 1)], terms_recv.at[step])
        total = terms[step, col]
        for k in range(1, n_cols):
            total = total + terms_in[step, near_x(k)]
        return total

    drain(gram_all.at[pl.ds(0, ring - 1)], gram_recv.at[3])
    gram_matrix = gram_all[...].reshape(gram.shape)

    def operator_rest(vector):
        return (
            jnp.dot(vector, gram_matrix, precision=highest, preferred_element_type=f32)
            + ridge * vector
        )

    solution = start[pl.ds(pl.multiple_of(col * quarter, quarter), quarter), :]
    residual = reduce_terms(0) - operator_rest(solution)
    direction = residual
    norm_now = jnp.sum(residual * residual, axis=1, keepdims=True)
    for iteration in range(ITERS):
        mine = direction_half.at[
            iteration, lax.div(col, block_quarters), lax.rem(col, block_quarters)
        ]
        mine[...] = direction.astype(bf16)
        for k in (2, 1, 3):
            remote(
                mine, mine, dir_send.at[iteration], dir_recv.at[iteration], row, near_x(k)
            ).start()
        rest = operator_rest(direction)
        drain(hub_xsum.at[pl.ds(0, dir_words)], dir_recv.at[iteration])

        groups(iteration + 1, direction_half.at[iteration], 0, tiles)
        applied = reduce_terms(iteration + 1) + rest
        step_size = norm_now / (jnp.sum(direction * applied, axis=1, keepdims=True) + tiny)
        solution = solution + step_size * direction
        residual = residual - step_size * applied
        norm_next = jnp.sum(residual * residual, axis=1, keepdims=True)
        direction = residual + norm_next / (norm_now + tiny) * direction
        norm_now = norm_next
    out_ref[0] = solution
    out_ref[1] = residual

    drain(asked_out.at[pl.ds(0, n_rows - 1)], asked_sem.at[0])
    drain(answers.at[pl.ds(0, n_rows - 1)], answer_send)
    drain(hub_x.at[pl.ds(0, n_cols - 1)], hub_send.at[0])
    drain(hub_y.at[pl.ds(0, ring - 1)], hub_send.at[1])
    drain(hub_z.at[pl.ds(0, planes - 1)], hub_send.at[2])
    drain(hub_y.at[pl.ds(0, ring // 2 - 1)], hub_send.at[3])
    drain(hub_x.at[pl.ds(0, n_cols - 1), pl.ds(0, per_col * halves)], hub_send.at[4])
    drain(hub_mine.at[pl.ds(0, n_cols // 2)], hub_send.at[5])
    drain(gram_y.at[pl.ds(0, ring - 1)], gram_send.at[0])
    drain(gram_x.at[pl.ds(0, n_cols - 1)], gram_send.at[1])
    drain(gram_z.at[pl.ds(0, planes - 1)], gram_send.at[2])
    drain(gram_all.at[pl.ds(0, ring - 1)], gram_send.at[3])
    for step in range(ITERS + 1):
        drain(terms_in.at[step, pl.ds(0, n_cols - 1)], terms_send.at[step])
    for iteration in range(ITERS):
        drain(hub_xsum.at[pl.ds(0, dir_words)], dir_send.at[iteration])


def per_device(
    n_rows,
    n_cols,
    mutant_factors,
    test_factors,
    weights,
    pattern,
    tile_block,
    hub_pick,
    hub_blocks,
    tail_req,
    tail_pick,
):
    mutant_rows, width = mutant_factors.shape
    tile = weights.shape[-1]
    tiles = weights.shape[2]
    hub_tiles = hub_pick.shape[2]
    hubs = hub_blocks.shape[0]
    cap = tail_req.shape[-1]
    full_rows = test_factors.shape[0]
    share = full_rows // n_cols
    slots = (tiles - hub_tiles) * tile
    ring = 8 if n_rows % 64 == 0 else 2
    planes = n_rows // ring
    per_col = hubs // n_cols
    piece = per_col * tile // ring
    gram_share = width // ring
    dims = (n_rows, n_cols, planes, ring, cap, tile, tiles, hub_tiles, hubs)
    vmem = pltpu.VMEM
    dma = pltpu.SemaphoreType.DMA
    scratch = [
        vmem((mutant_rows // tile, tile, width), bf16),
        vmem((mutant_rows, width), f32),
        vmem((full_rows, width), f32),
        vmem((tiles, tile, tile), bf16),
        vmem((tiles, tile, tile), jnp.int32),
        vmem((tiles, tile, tile), bf16),
        vmem((n_rows, cap), jnp.int32),
        pltpu.SMEM((slots,), jnp.int32),
        vmem((n_rows, 1, 128), jnp.int32),
        vmem((n_rows, 1, 128), jnp.int32),
        pltpu.SMEM((n_rows, 1, 128), jnp.int32),
        vmem((cap, width), f32),
        vmem((n_rows, cap, width), bf16),
        vmem((n_rows, cap, width), bf16),
        vmem((slots, width), f32),
        vmem((tile, width), f32),
        vmem((tiles, tile, width), bf16),
        vmem((n_cols, ring, piece, width), bf16),
        vmem((n_cols, ring, piece, width), bf16),
        vmem((ring, piece, width), bf16),
        vmem((ring, piece, width), bf16),
        vmem((piece, width), bf16),
        vmem((planes, piece, width), bf16),
        vmem((per_col, ring // per_col // 2, piece, width), bf16),
        vmem((hubs, 2, ring // per_col // 2, piece, width), bf16),
        vmem((ring, gram_share, width), f32),
        vmem((n_cols, gram_share, width), f32),
        vmem((gram_share, width), f32),
        vmem((ring, gram_share, width), f32),
        vmem((gram_share, width), f32),
        vmem((planes, gram_share, width), f32),
        vmem((ring, gram_share, width), f32),
        vmem((2, n_cols // 2, share, width), bf16),
        vmem((ITERS, 2, n_cols // 2, share, width), bf16),
        vmem((ITERS + 1, n_cols, share, width), f32),
        vmem((ITERS + 1, n_cols, share, width), f32),
        dma((7,)),
        dma((2,)),
        dma,
        dma((n_rows,)),
        dma((6,)),
        dma((6,)),
        dma((4,)),
        dma((4,)),
        dma((ITERS + 1,)),
        dma((ITERS + 1,)),
        dma((ITERS,)),
        dma((ITERS,)),
    ]
    anywhere = pl.BlockSpec(memory_space=pl.ANY)
    scalars = pl.BlockSpec(memory_space=pltpu.SMEM)
    both = pl.pallas_call(
        functools.partial(kernel, dims),
        out_shape=jax.ShapeDtypeStruct((2, share, width), f32),
        in_specs=[anywhere] * 6 + [scalars] * 3,
        out_specs=pl.BlockSpec(memory_space=vmem),
        scratch_shapes=scratch,
        compiler_params=pltpu.CompilerParams(
            collective_id=0, has_side_effects=True, vmem_limit_bytes=56 * 1024 * 1024
        ),
    )(
        mutant_factors.reshape(-1, tile, width),
        test_factors,
        weights.reshape(weights.shape[2:]),
        pattern.reshape(pattern.shape[2:]),
        tail_req.reshape(tail_req.shape[2:]),
        tail_pick.reshape(slots),
        tile_block.reshape(tiles),
        hub_pick.reshape(hub_tiles),
        hub_blocks,
    )
    return both[0], both[1]


def solution(mesh):
    in_specs = (
        P(("rows", "cols"), None),
        P("rows", None),
        P("rows", "cols", None, None, None),
        P("rows", "cols", None, None, None),
        P("rows", "cols", None),
        P("rows", "cols", None),
        P(),
        P("rows", "cols", None, None),
        P("rows", "cols", None),
    )
    out_specs = (P(("rows", "cols"), None), P(("rows", "cols"), None))
    return jax.shard_map(
        functools.partial(per_device, mesh.shape["rows"], mesh.shape["cols"]),
        mesh=mesh,
        in_specs=in_specs,
        out_specs=out_specs,
        check_vma=False,
    )
```

```python
import functools

import jax
import jax.numpy as jnp
from jax import lax
from jax.experimental import pallas as pl
from jax.experimental.pallas import tpu as pltpu
from jax.sharding import PartitionSpec as P

ITERS = 2
GROUP = 4
LATER = 14

ridge = 0.1
tiny = 1e-06
highest = lax.Precision.HIGHEST
f32 = jnp.float32
bf16 = jnp.bfloat16


def fold(a, b):
    return lax.dot_general(a, b, (((0,), (0,)), ((), ())), preferred_element_type=f32)


def across(a, b):
    return lax.dot_general(a, b, (((1,), (1,)), ((), ())), preferred_element_type=f32)


def plain(a, b):
    return jnp.dot(a, b, preferred_element_type=f32)


def remote(src, dst, send_sem, recv_sem, row, col):
    return pltpu.make_async_remote_copy(
        src_ref=src,
        dst_ref=dst,
        send_sem=send_sem,
        recv_sem=recv_sem,
        device_id=(row, col),
        device_id_type=pl.DeviceIdType.MESH,
    )


def drain(ref, sem):
    pltpu.make_async_copy(ref, ref, sem).wait()


def kernel(
    dims,
    mutants_h,
    start_h,
    weights_h,
    pattern_h,
    requests_h,
    pick_h,
    block_s,
    hub_pick_s,
    hub_block_s,
    out_ref,
    mutants,
    mutants32,
    start,
    weights,
    pattern,
    confidence,
    requests,
    pick_s,
    asked_out,
    asked_in,
    asked_s,
    rows32,
    answers,
    received,
    tail32,
    tile32,
    factors,
    hub_mine,
    hub_x,
    hub_xsum,
    hub_y,
    hub_ysum,
    hub_z,
    hub_share,
    hub_all,
    gram_mine,
    gram_x,
    gram_xsum,
    gram_y,
    gram_ysum,
    gram_z,
    gram_all,
    start_half,
    direction_half,
    terms,
    terms_in,
    local_sem,
    asked_sem,
    answer_send,
    answer_recv,
    hub_send,
    hub_recv,
    gram_send,
    gram_recv,
    terms_send,
    terms_recv,
    dir_send,
    dir_recv,
):
    n_rows, n_cols, planes, ring, cap, tile, tiles, hub_tiles, hubs = dims
    row = lax.axis_index("rows")
    col = lax.axis_index("cols")
    z = lax.div(row, ring)
    yc = lax.rem(row, ring)
    tail_tiles = tiles - hub_tiles

    def near_x(k):
        return lax.rem(col + k, n_cols)

    def near_y(k):
        return lax.rem(yc + k, ring)

    def near_z(k):
        return lax.rem(z + k, planes)

    def partner(i):
        k = lax.rem(i, planes)
        half = lax.div(k + 1, 2)
        dz = planes // 2 + half * (1 - 2 * lax.rem(k, 2))
        dy = lax.div(i, planes) + 1
        return lax.rem(z + dz, planes) * ring + lax.rem(yc + dy, ring)

    dir_words = (n_cols - 1) * (start.shape[0] // n_cols) // hub_ysum.shape[0]

    local = [
        pltpu.make_async_copy(requests_h, requests, local_sem.at[0]),
        pltpu.make_async_copy(mutants_h, mutants, local_sem.at[1]),
        pltpu.make_async_copy(pick_h, pick_s, local_sem.at[2]),
        pltpu.make_async_copy(start_h, start, local_sem.at[3]),
        pltpu.make_async_copy(weights_h, weights, local_sem.at[4]),
        pltpu.make_async_copy(pattern_h, pattern, local_sem.at[5]),
    ]
    for copy in local:
        copy.start()

    barrier = pltpu.get_barrier_semaphore()

    def greet(i, carry):
        pl.semaphore_signal(
            barrier, inc=1, device_id=(partner(i), col), device_id_type=pl.DeviceIdType.MESH
        )
        return carry

    lax.fori_loop(0, n_rows - 1, greet, 0)
    for k in range(1, n_cols):
        pl.semaphore_signal(
            barrier, inc=1, device_id=(row, near_x(k)), device_id_type=pl.DeviceIdType.MESH
        )
    local[0].wait()
    for o in range(n_rows):
        asked_out[o, :, 0:cap] = requests[o : o + 1, :]
    pl.semaphore_wait(barrier, n_rows + n_cols - 2)

    def ask(i, carry):
        d = partner(i)
        remote(asked_out.at[d], asked_in.at[row], asked_sem.at[0], asked_sem.at[1], d, col).start()
        return carry

    lax.fori_loop(0, n_rows - 1, ask, 0)
    asked_in[row] = asked_out[row]

    local[1].wait()
    blocks_here = mutants.shape[0]
    for o in range(blocks_here):
        mutants32[o * tile : (o + 1) * tile] = mutants[o].astype(f32)
    me = row * n_cols + col
    per_col = hubs // n_cols
    pieces = ring // per_col
    for h in range(hubs):
        block = hub_block_s[h]
        own = mutants[lax.rem(block, blocks_here)]
        owner = jnp.full(own.shape, lax.div(block, blocks_here), jnp.int32)
        kept = jnp.where(owner == me, own.astype(f32), 0.0).astype(bf16)
        at = slice(h % per_col * pieces, (h % per_col + 1) * pieces)
        hub_mine[h // per_col, at] = kept.reshape(pieces, tile // pieces, kept.shape[-1])

    def send_hub_x(p):
        q = near_x(lax.rem(p, n_cols - 1) + 1)
        e = lax.div(p, n_cols - 1)
        remote(
            hub_mine.at[q, e], hub_x.at[col, e], hub_send.at[0], hub_recv.at[0], row, q
        ).start()

    hub_pieces = (n_cols - 1) * ring
    early = hub_pieces // 3
    for p in range(early):
        send_hub_x(p)

    drain(asked_in.at[pl.ds(0, n_rows - 1)], asked_sem.at[1])
    fetch = pltpu.make_async_copy(asked_in, asked_s, local_sem.at[6])
    fetch.start()
    fetch.wait()

    def gather_for(d):
        for j in range(cap):
            rows32[j : j + 1, :] = mutants32[pl.ds(asked_s[d, 0, j], 1), :]
        return rows32[...].astype(bf16)

    def serve(i, carry):
        d = partner(i)
        answers[i] = gather_for(d)
        remote(
            answers.at[i], received.at[row], answer_send, answer_recv.at[row], d, col
        ).start()
        return carry

    def prepare(n, carry):
        w = weights[n].astype(f32)
        p = pattern[n].astype(f32)
        weights[n] = (w * p).astype(bf16)
        confidence[n] = (p * (1.0 + w)).astype(bf16)
        return carry

    others = n_rows - 1
    def serve_and_send(i, carry):
        serve(i, carry)
        send_hub_x(early + i)
        return carry

    def serve_and_send(i, carry):
        serve(i, carry)
        send_hub_x(early + i)
        return carry

    cuts = [hub_pieces - early, others * 4 // 9, others * 2 // 3]
    ready = [tiles * c // 4 for c in range(5)]

    first_cut = hub_pieces - early
    cuts = [first_cut] + [first_cut + (others - first_cut) * c // 47 for c in (12, 26)]
    ready = [tiles * c // 3 for c in range(4)]

    lax.fori_loop(0, cuts[0], serve_and_send, 0)
    rows_here = mutants[...].reshape(mutants32.shape)
    gram = fold(rows_here, rows_here)
    share = gram_mine.shape[1]
    for q in range(ring):
        gram_mine[q] = gram[q * share : (q + 1) * share]
    for k in range(1, ring):
        e = near_y(k)
        remote(
            gram_mine.at[e], gram_y.at[yc], gram_send.at[0], gram_recv.at[0], z * ring + e, col
        ).start()
    lax.fori_loop(cuts[0], cuts[1], serve, 0)
    local[4].wait()
    local[5].wait()
    lax.fori_loop(ready[0], ready[1], prepare, 0)

    drain(hub_x.at[pl.ds(0, n_cols - 1)], hub_recv.at[0])
    total = hub_mine[col]
    for k in range(1, n_cols):
        total = total + hub_x[near_x(k)]
    hub_xsum[...] = total
    for k in range(1, ring):
        e = near_y(k)
        remote(
            hub_xsum.at[e], hub_y.at[yc], hub_send.at[1], hub_recv.at[1], z * ring + e, col
        ).start()
    drain(gram_y.at[pl.ds(0, ring - 1)], gram_recv.at[0])
    gsum = gram_mine[yc]
    for k in range(1, ring):
        gsum = gsum + gram_y[near_y(k)]
    gram_ysum[...] = gsum
    for k in range(1, n_cols):
        remote(
            gram_ysum, gram_x.at[col], gram_send.at[1], gram_recv.at[1], row, near_x(k)
        ).start()
    lax.fori_loop(cuts[1], cuts[2], serve, 0)
    lax.fori_loop(ready[1], ready[2], prepare, 0)

    drain(hub_y.at[pl.ds(0, ring - 1)], hub_recv.at[1])
    total = hub_xsum[yc]
    for k in range(1, ring):
        total = total + hub_y[near_y(k)]
    hub_ysum[...] = total
    for k in range(1, planes):
        e = near_z(k)
        remote(
            hub_ysum, hub_z.at[z], hub_send.at[2], hub_recv.at[2], e * ring + yc, col
        ).start()
    drain(gram_x.at[pl.ds(0, n_cols - 1)], gram_recv.at[1])
    gsum = gram_ysum[...]
    for k in range(1, n_cols):
        gsum = gsum + gram_x[near_x(k)]
    gram_xsum[...] = gsum
    lax.fori_loop(cuts[2], others, serve, 0)
    for k in range(1, planes):
        e = near_z(k)
        remote(
            gram_xsum, gram_z.at[z], gram_send.at[2], gram_recv.at[2], e * ring + yc, col
        ).start()
    lax.fori_loop(ready[2], ready[3], prepare, 0)
    received[row] = gather_for(row)
    local[3].wait()
    quarter = start.shape[0] // n_cols
    block_quarters = tile // quarter
    for q in range(n_cols):
        start_half[q // block_quarters, q % block_quarters] = start[
            q * quarter : (q + 1) * quarter
        ].astype(bf16)
    for step in range(ITERS + 1):
        terms[step] = jnp.zeros(terms.shape[1:], f32)

    slab = quarter // 2

    def group(step, vector, m, base, size):
        parts = []
        for u in range(size):
            n = base + u
            b = block_s[n]
            v = vector[b][:, m * slab : (m + 1) * slab].reshape(tile // 2, factors.shape[-1])
            scores = across(v, factors[n])
            w = jnp.concatenate(
                [weights[n, q * quarter + m * slab : q * quarter + (m + 1) * slab]
                 for q in range(block_quarters)]
            )
            parts.append((n, b, (scores * w.astype(f32)).astype(bf16)))
        sums = [None, None]
        for n, b, weighted in parts:
            product = plain(weighted, factors[n])
            if step == 0:
                c = jnp.concatenate(
                    [confidence[n, q * quarter + m * slab : q * quarter + (m + 1) * slab]
                     for q in range(block_quarters)]
                )
                product = plain(c, factors[n]) - product
            covers = jnp.full(product.shape, b, jnp.int32)
            for half in range(2):
                kept = jnp.where(covers == half, product, 0.0)
                sums[half] = kept if sums[half] is None else sums[half] + kept
        for half in range(2):
            for q in range(block_quarters):
                terms[step, half * block_quarters + q, m * slab : (m + 1) * slab] += sums[half][
                    q * slab : (q + 1) * slab
                ]

    def groups(step, vector, m, first, last, size):
        def one(g, carry):
            group(step, vector, m, g * size, size)
            return carry

        lax.fori_loop(first // size, last // size, one, 0)

    def send_terms(step, m):
        at = pl.ds(m * slab, slab)
        for k in (2, 1, 3):
            q = near_x(k)
            remote(
                terms.at[step, q, at], terms_in.at[step, col, at],
                terms_send.at[step, m], terms_recv.at[step, m], row, q,
            ).start()

    def arrive(i, carry):
        o = partner(i)
        remote(
            answers.at[i], received.at[o], answer_send, answer_recv.at[o], o, col
        ).wait_recv()
        tail32[pl.ds(pl.multiple_of(o * cap, cap), cap), :] = received[o].astype(f32)
        return carry

    lax.fori_loop(0, cuts[2], arrive, 0)

    drain(hub_z.at[pl.ds(0, planes - 1)], hub_recv.at[2])
    total = hub_ysum[...]
    for k in range(1, planes):
        total = total + hub_z[near_z(k)]
    core = lax.rem(yc, 2)
    my_piece = hub_share.at[lax.div(yc, pieces), lax.div(lax.rem(yc, pieces), 2)]
    my_piece[...] = total
    for k in range(2, ring, 2):
        remote(
            my_piece, my_piece, hub_send.at[3], hub_recv.at[3], z * ring + near_y(k), col
        ).start()
    lax.fori_loop(cuts[2], others, arrive, 0)
    tail32[pl.ds(pl.multiple_of(row * cap, cap), cap), :] = received[row].astype(f32)

    def tail_tile(l, carry):
        for i in range(tile):
            tile32[i : i + 1, :] = tail32[pl.ds(pick_s[l * tile + i], 1), :]
        factors[l + hub_tiles] = tile32[...].astype(bf16)
        return carry

    local[2].wait()

    drain(hub_y.at[pl.ds(0, ring // 2 - 1)], hub_recv.at[3])
    halves = pieces // 2
    for h in range(per_col):
        at = col * per_col + h
        for k in (2, 1, 3):
            remote(
                hub_share.at[h], hub_all.at[at, core],
                hub_send.at[4], hub_recv.at[4], row, near_x(k),
            ).start()
        hub_all[at, core] = hub_share[h]

    drain(gram_z.at[pl.ds(0, planes - 1)], gram_recv.at[2])
    gsum = gram_xsum[...]
    for k in range(1, planes):
        gsum = gsum + gram_z[near_z(k)]
    gram_all[yc] = gsum
    for k in range(1, ring):
        remote(
            gram_all.at[yc], gram_all.at[yc], gram_send.at[3], gram_recv.at[3],
            z * ring + near_y(k), col,
        ).start()
    middle = tail_tiles * 3 // 4
    lax.fori_loop(0, middle, tail_tile, 0)

    drain(hub_x.at[pl.ds(0, n_cols - 1), pl.ds(0, per_col * halves)], hub_recv.at[4])
    sibling = row + 1 - 2 * core
    for h in range(hubs):
        remote(
            hub_all.at[h, core], hub_all.at[h, core],
            hub_send.at[5], hub_recv.at[5], sibling, col,
        ).start()
    lax.fori_loop(middle, tail_tiles, tail_tile, 0)
    groups(0, start_half, 0, hub_tiles, tiles, GROUP)
    drain(hub_mine.at[pl.ds(0, n_cols // 2)], hub_recv.at[5])
    for n in range(hub_tiles):
        part = hub_all[hub_pick_s[n]]
        for m in range(halves):
            for c in range(2):
                at = (2 * m + c) * part.shape[2]
                factors[n, at : at + part.shape[2]] = part[c, m]
    groups(0, start_half, 0, 0, hub_tiles, 2 * GROUP)
    send_terms(0, 0)
    groups(0, start_half, 1, 0, tiles, LATER // 2)
    send_terms(0, 1)

    def reduce_terms(step):
        for m in range(2):
            drain(
                terms_in.at[step, pl.ds(0, n_cols - 1), pl.ds(0, slab)], terms_recv.at[step, m]
            )
        total = terms[step, col]
        for k in range(1, n_cols):
            total = total + terms_in[step, near_x(k)]
        return total

    drain(gram_all.at[pl.ds(0, ring - 1)], gram_recv.at[3])
    gram_matrix = gram_all[...].reshape(gram.shape)

    def operator_rest(vector):
        return (
            jnp.dot(vector, gram_matrix, precision=highest, preferred_element_type=f32)
            + ridge * vector
        )

    solution = start[pl.ds(pl.multiple_of(col * quarter, quarter), quarter), :]
    residual = reduce_terms(0) - operator_rest(solution)
    direction = residual
    norm_now = jnp.sum(residual * residual, axis=1, keepdims=True)
    for iteration in range(ITERS):
        mine = direction_half.at[
            iteration, lax.div(col, block_quarters), lax.rem(col, block_quarters)
        ]
        mine[...] = direction.astype(bf16)
        for k in (2, 1, 3):
            remote(
                mine, mine, dir_send.at[iteration], dir_recv.at[iteration], row, near_x(k)
            ).start()
        rest = operator_rest(direction)
        drain(hub_xsum.at[pl.ds(0, dir_words)], dir_recv.at[iteration])

        for m in range(2):
            groups(iteration + 1, direction_half.at[iteration], m, 0, tiles, LATER)
            send_terms(iteration + 1, m)
        applied = reduce_terms(iteration + 1) + rest
        step_size = norm_now / (jnp.sum(direction * applied, axis=1, keepdims=True) + tiny)
        solution = solution + step_size * direction
        residual = residual - step_size * applied
        norm_next = jnp.sum(residual * residual, axis=1, keepdims=True)
        direction = residual + norm_next / (norm_now + tiny) * direction
        norm_now = norm_next
    out_ref[0] = solution
    out_ref[1] = residual

    drain(asked_out.at[pl.ds(0, n_rows - 1)], asked_sem.at[0])
    drain(answers.at[pl.ds(0, n_rows - 1)], answer_send)
    drain(hub_x.at[pl.ds(0, n_cols - 1)], hub_send.at[0])
    drain(hub_y.at[pl.ds(0, ring - 1)], hub_send.at[1])
    drain(hub_z.at[pl.ds(0, planes - 1)], hub_send.at[2])
    drain(hub_y.at[pl.ds(0, ring // 2 - 1)], hub_send.at[3])
    drain(hub_x.at[pl.ds(0, n_cols - 1), pl.ds(0, per_col * halves)], hub_send.at[4])
    drain(hub_mine.at[pl.ds(0, n_cols // 2)], hub_send.at[5])
    drain(gram_y.at[pl.ds(0, ring - 1)], gram_send.at[0])
    drain(gram_x.at[pl.ds(0, n_cols - 1)], gram_send.at[1])
    drain(gram_z.at[pl.ds(0, planes - 1)], gram_send.at[2])
    drain(gram_all.at[pl.ds(0, ring - 1)], gram_send.at[3])
    for step in range(ITERS + 1):
        for m in range(2):
            drain(
                terms_in.at[step, pl.ds(0, n_cols - 1), pl.ds(0, slab)], terms_send.at[step, m]
            )
    for iteration in range(ITERS):
        drain(hub_xsum.at[pl.ds(0, dir_words)], dir_send.at[iteration])


def per_device(
    n_rows,
    n_cols,
    mutant_factors,
    test_factors,
    weights,
    pattern,
    tile_block,
    hub_pick,
    hub_blocks,
    tail_req,
    tail_pick,
):
    mutant_rows, width = mutant_factors.shape
    tile = weights.shape[-1]
    tiles = weights.shape[2]
    hub_tiles = hub_pick.shape[2]
    hubs = hub_blocks.shape[0]
    cap = tail_req.shape[-1]
    full_rows = test_factors.shape[0]
    share = full_rows // n_cols
    slots = (tiles - hub_tiles) * tile
    ring = 8 if n_rows % 64 == 0 else 2
    planes = n_rows // ring
    per_col = hubs // n_cols
    piece = per_col * tile // ring
    gram_share = width // ring
    dims = (n_rows, n_cols, planes, ring, cap, tile, tiles, hub_tiles, hubs)
    vmem = pltpu.VMEM
    dma = pltpu.SemaphoreType.DMA
    scratch = [
        vmem((mutant_rows // tile, tile, width), bf16),
        vmem((mutant_rows, width), f32),
        vmem((full_rows, width), f32),
        vmem((tiles, tile, tile), bf16),
        vmem((tiles, tile, tile), jnp.int32),
        vmem((tiles, tile, tile), bf16),
        vmem((n_rows, cap), jnp.int32),
        pltpu.SMEM((slots,), jnp.int32),
        vmem((n_rows, 1, 128), jnp.int32),
        vmem((n_rows, 1, 128), jnp.int32),
        pltpu.SMEM((n_rows, 1, 128), jnp.int32),
        vmem((cap, width), f32),
        vmem((n_rows, cap, width), bf16),
        vmem((n_rows, cap, width), bf16),
        vmem((slots, width), f32),
        vmem((tile, width), f32),
        vmem((tiles, tile, width), bf16),
        vmem((n_cols, ring, piece, width), bf16),
        vmem((n_cols, ring, piece, width), bf16),
        vmem((ring, piece, width), bf16),
        vmem((ring, piece, width), bf16),
        vmem((piece, width), bf16),
        vmem((planes, piece, width), bf16),
        vmem((per_col, ring // per_col // 2, piece, width), bf16),
        vmem((hubs, 2, ring // per_col // 2, piece, width), bf16),
        vmem((ring, gram_share, width), f32),
        vmem((n_cols, gram_share, width), f32),
        vmem((gram_share, width), f32),
        vmem((ring, gram_share, width), f32),
        vmem((gram_share, width), f32),
        vmem((planes, gram_share, width), f32),
        vmem((ring, gram_share, width), f32),
        vmem((2, n_cols // 2, share, width), bf16),
        vmem((ITERS, 2, n_cols // 2, share, width), bf16),
        vmem((ITERS + 1, n_cols, share, width), f32),
        vmem((ITERS + 1, n_cols, share, width), f32),
        dma((7,)),
        dma((2,)),
        dma,
        dma((n_rows,)),
        dma((6,)),
        dma((6,)),
        dma((4,)),
        dma((4,)),
        dma((ITERS + 1, 2)),
        dma((ITERS + 1, 2)),
        dma((ITERS,)),
        dma((ITERS,)),
    ]
    anywhere = pl.BlockSpec(memory_space=pl.ANY)
    scalars = pl.BlockSpec(memory_space=pltpu.SMEM)
    both = pl.pallas_call(
        functools.partial(kernel, dims),
        out_shape=jax.ShapeDtypeStruct((2, share, width), f32),
        in_specs=[anywhere] * 6 + [scalars] * 3,
        out_specs=pl.BlockSpec(memory_space=vmem),
        scratch_shapes=scratch,
        compiler_params=pltpu.CompilerParams(
            collective_id=0, has_side_effects=True, vmem_limit_bytes=56 * 1024 * 1024
        ),
    )(
        mutant_factors.reshape(-1, tile, width),
        test_factors,
        weights.reshape(weights.shape[2:]),
        pattern.reshape(pattern.shape[2:]),
        tail_req.reshape(tail_req.shape[2:]),
        tail_pick.reshape(slots),
        tile_block.reshape(tiles),
        hub_pick.reshape(hub_tiles),
        hub_blocks,
    )
    return both[0], both[1]


def solution(mesh):
    in_specs = (
        P(("rows", "cols"), None),
        P("rows", None),
        P("rows", "cols", None, None, None),
        P("rows", "cols", None, None, None),
        P("rows", "cols", None),
        P("rows", "cols", None),
        P(),
        P("rows", "cols", None, None),
        P("rows", "cols", None),
    )
    out_specs = (P(("rows", "cols"), None), P(("rows", "cols"), None))
    return jax.shard_map(
        functools.partial(per_device, mesh.shape["rows"], mesh.shape["cols"]),
        mesh=mesh,
        in_specs=in_specs,
        out_specs=out_specs,
        check_vma=False,
    )
```

```python
import functools

import jax
import jax.numpy as jnp
from jax import lax
from jax.experimental import pallas as pl
from jax.experimental.pallas import tpu as pltpu
from jax.sharding import PartitionSpec as P

ITERS = 2
FIRST = 10
LATER = 14

ridge = 0.1
tiny = 1e-06
highest = lax.Precision.HIGHEST
f32 = jnp.float32
bf16 = jnp.bfloat16


def fold(a, b):
    return lax.dot_general(a, b, (((0,), (0,)), ((), ())), preferred_element_type=f32)


def across(a, b):
    return lax.dot_general(a, b, (((1,), (1,)), ((), ())), preferred_element_type=f32)


def plain(a, b):
    return jnp.dot(a, b, preferred_element_type=f32)


def remote(src, dst, send_sem, recv_sem, row, col):
    return pltpu.make_async_remote_copy(
        src_ref=src,
        dst_ref=dst,
        send_sem=send_sem,
        recv_sem=recv_sem,
        device_id=(row, col),
        device_id_type=pl.DeviceIdType.MESH,
    )


def drain(ref, sem):
    pltpu.make_async_copy(ref, ref, sem).wait()


def kernel(
    dims,
    mutants_h,
    start_h,
    weights_h,
    pattern_h,
    requests_h,
    pick_h,
    block_s,
    hub_pick_s,
    hub_block_s,
    out_ref,
    mutants,
    mutants32,
    start,
    weights,
    pattern,
    confidence,
    requests,
    pick_s,
    asked_out,
    asked_in,
    asked_s,
    rows32,
    answers,
    received,
    tail32,
    tile32,
    factors,
    hub_mine,
    hub_x,
    hub_xsum,
    hub_y,
    hub_ysum,
    hub_z,
    hub_share,
    hub_all,
    gram_mine,
    gram_x,
    gram_xsum,
    gram_y,
    gram_ysum,
    gram_z,
    gram_all,
    start_half,
    direction_half,
    terms,
    terms_in,
    local_sem,
    asked_sem,
    answer_send,
    answer_recv,
    hub_send,
    hub_recv,
    gram_send,
    gram_recv,
    terms_send,
    terms_recv,
    dir_send,
    dir_recv,
):
    n_rows, n_cols, planes, ring, cap, tile, tiles, hub_tiles, hubs = dims
    row = lax.axis_index("rows")
    col = lax.axis_index("cols")
    z = lax.div(row, ring)
    yc = lax.rem(row, ring)
    tail_tiles = tiles - hub_tiles

    def near_x(k):
        return lax.rem(col + k, n_cols)

    def near_y(k):
        return lax.rem(yc + k, ring)

    def near_z(k):
        return lax.rem(z + k, planes)

    def partner(i):
        k = lax.rem(i, planes)
        half = lax.div(k + 1, 2)
        dz = planes // 2 + half * (1 - 2 * lax.rem(k, 2))
        dy = lax.div(i, planes) + 1
        return lax.rem(z + dz, planes) * ring + lax.rem(yc + dy, ring)

    dir_words = (n_cols - 1) * (start.shape[0] // n_cols) // hub_ysum.shape[0]

    local = [
        pltpu.make_async_copy(requests_h, requests, local_sem.at[0]),
        pltpu.make_async_copy(mutants_h, mutants, local_sem.at[1]),
        pltpu.make_async_copy(pick_h, pick_s, local_sem.at[2]),
        pltpu.make_async_copy(start_h, start, local_sem.at[3]),
        pltpu.make_async_copy(weights_h, weights, local_sem.at[4]),
        pltpu.make_async_copy(pattern_h, pattern, local_sem.at[5]),
    ]
    for copy in local:
        copy.start()

    barrier = pltpu.get_barrier_semaphore()

    def greet(i, carry):
        pl.semaphore_signal(
            barrier, inc=1, device_id=(partner(i), col), device_id_type=pl.DeviceIdType.MESH
        )
        return carry

    lax.fori_loop(0, n_rows - 1, greet, 0)
    for k in range(1, n_cols):
        pl.semaphore_signal(
            barrier, inc=1, device_id=(row, near_x(k)), device_id_type=pl.DeviceIdType.MESH
        )
    local[0].wait()
    for o in range(n_rows):
        asked_out[o, :, 0:cap] = requests[o : o + 1, :]
    pl.semaphore_wait(barrier, n_rows + n_cols - 2)

    def ask(i, carry):
        d = partner(i)
        remote(asked_out.at[d], asked_in.at[row], asked_sem.at[0], asked_sem.at[1], d, col).start()
        return carry

    lax.fori_loop(0, n_rows - 1, ask, 0)
    asked_in[row] = asked_out[row]

    local[1].wait()
    blocks_here = mutants.shape[0]
    for o in range(blocks_here):
        mutants32[o * tile : (o + 1) * tile] = mutants[o].astype(f32)
    me = row * n_cols + col
    per_col = hubs // n_cols
    pieces = ring // per_col
    for h in range(hubs):
        block = hub_block_s[h]
        own = mutants[lax.rem(block, blocks_here)]
        owner = jnp.full(own.shape, lax.div(block, blocks_here), jnp.int32)
        kept = jnp.where(owner == me, own.astype(f32), 0.0).astype(bf16)
        at = slice(h % per_col * pieces, (h % per_col + 1) * pieces)
        hub_mine[h // per_col, at] = kept.reshape(pieces, tile // pieces, kept.shape[-1])

    def send_hub_x(p):
        q = near_x(lax.rem(p, n_cols - 1) + 1)
        e = lax.div(p, n_cols - 1)
        remote(
            hub_mine.at[q, e], hub_x.at[col, e], hub_send.at[0], hub_recv.at[0], row, q
        ).start()

    hub_pieces = (n_cols - 1) * ring
    early = hub_pieces // 3
    for p in range(early):
        send_hub_x(p)

    drain(asked_in.at[pl.ds(0, n_rows - 1)], asked_sem.at[1])
    fetch = pltpu.make_async_copy(asked_in, asked_s, local_sem.at[6])
    fetch.start()
    fetch.wait()

    def gather_for(d):
        for j in range(cap):
            rows32[j : j + 1, :] = mutants32[pl.ds(asked_s[d, 0, j], 1), :]
        return rows32[...].astype(bf16)

    def serve(i, carry):
        d = partner(i)
        answers[i] = gather_for(d)
        remote(
            answers.at[i], received.at[row], answer_send, answer_recv.at[row], d, col
        ).start()
        return carry

    def prepare(n, carry):
        w = weights[n].astype(f32)
        p = pattern[n].astype(f32)
        weights[n] = (w * p).astype(bf16)
        confidence[n] = (p * (1.0 + w)).astype(bf16)
        return carry

    others = n_rows - 1
    def serve_and_send(i, carry):
        serve(i, carry)
        send_hub_x(early + i)
        return carry

    def serve_and_send(i, carry):
        serve(i, carry)
        send_hub_x(early + i)
        return carry

    cuts = [hub_pieces - early, others * 4 // 9, others * 2 // 3]
    ready = [tiles * c // 4 for c in range(5)]

    first_cut = hub_pieces - early
    cuts = [first_cut] + [first_cut + (others - first_cut) * c // 47 for c in (12, 26)]
    ready = [tiles * c // 3 for c in range(4)]

    lax.fori_loop(0, cuts[0], serve_and_send, 0)
    rows_here = mutants[...].reshape(mutants32.shape)
    gram = fold(rows_here, rows_here)
    share = gram_mine.shape[1]
    for q in range(ring):
        gram_mine[q] = gram[q * share : (q + 1) * share]
    for k in range(1, ring):
        e = near_y(k)
        remote(
            gram_mine.at[e], gram_y.at[yc], gram_send.at[0], gram_recv.at[0], z * ring + e, col
        ).start()
    lax.fori_loop(cuts[0], cuts[1], serve, 0)
    local[4].wait()
    local[5].wait()
    lax.fori_loop(ready[0], ready[1], prepare, 0)

    drain(hub_x.at[pl.ds(0, n_cols - 1)], hub_recv.at[0])
    total = hub_mine[col]
    for k in range(1, n_cols):
        total = total + hub_x[near_x(k)]
    hub_xsum[...] = total
    for k in range(1, ring):
        e = near_y(k)
        remote(
            hub_xsum.at[e], hub_y.at[yc], hub_send.at[1], hub_recv.at[1], z * ring + e, col
        ).start()
    drain(gram_y.at[pl.ds(0, ring - 1)], gram_recv.at[0])
    gsum = gram_mine[yc]
    for k in range(1, ring):
        gsum = gsum + gram_y[near_y(k)]
    gram_ysum[...] = gsum
    for k in range(1, n_cols):
        remote(
            gram_ysum, gram_x.at[col], gram_send.at[1], gram_recv.at[1], row, near_x(k)
        ).start()
    lax.fori_loop(cuts[1], cuts[2], serve, 0)
    lax.fori_loop(ready[1], ready[2], prepare, 0)

    drain(hub_y.at[pl.ds(0, ring - 1)], hub_recv.at[1])
    total = hub_xsum[yc]
    for k in range(1, ring):
        total = total + hub_y[near_y(k)]
    hub_ysum[...] = total
    for k in range(1, planes):
        e = near_z(k)
        remote(
            hub_ysum, hub_z.at[z], hub_send.at[2], hub_recv.at[2], e * ring + yc, col
        ).start()
    drain(gram_x.at[pl.ds(0, n_cols - 1)], gram_recv.at[1])
    gsum = gram_ysum[...]
    for k in range(1, n_cols):
        gsum = gsum + gram_x[near_x(k)]
    gram_xsum[...] = gsum
    lax.fori_loop(cuts[2], others, serve, 0)
    for k in range(1, planes):
        e = near_z(k)
        remote(
            gram_xsum, gram_z.at[z], gram_send.at[2], gram_recv.at[2], e * ring + yc, col
        ).start()
    lax.fori_loop(ready[2], ready[3], prepare, 0)
    received[row] = gather_for(row)
    local[3].wait()
    quarter = start.shape[0] // n_cols
    block_quarters = tile // quarter
    for q in range(n_cols):
        start_half[q // block_quarters, q % block_quarters] = start[
            q * quarter : (q + 1) * quarter
        ].astype(bf16)
    for step in range(ITERS + 1):
        terms[step] = jnp.zeros(terms.shape[1:], f32)

    slab = quarter // 2

    def group(step, vector, m, base, size):
        parts = []
        for u in range(size):
            n = base + u
            b = block_s[n]
            v = vector[b][:, m * slab : (m + 1) * slab].reshape(tile // 2, factors.shape[-1])
            scores = across(v, factors[n])
            w = jnp.concatenate(
                [weights[n, q * quarter + m * slab : q * quarter + (m + 1) * slab]
                 for q in range(block_quarters)]
            )
            parts.append((n, b, (scores * w.astype(f32)).astype(bf16)))
        sums = [None, None]
        for n, b, weighted in parts:
            product = plain(weighted, factors[n])
            if step == 0:
                c = jnp.concatenate(
                    [confidence[n, q * quarter + m * slab : q * quarter + (m + 1) * slab]
                     for q in range(block_quarters)]
                )
                product = plain(c, factors[n]) - product
            covers = jnp.full(product.shape, b, jnp.int32)
            for half in range(2):
                kept = jnp.where(covers == half, product, 0.0)
                sums[half] = kept if sums[half] is None else sums[half] + kept
        for half in range(2):
            for q in range(block_quarters):
                terms[step, half * block_quarters + q, m * slab : (m + 1) * slab] += sums[half][
                    q * slab : (q + 1) * slab
                ]

    def groups(step, vector, m, first, last, size):
        def one(g, carry):
            group(step, vector, m, first + g * size, size)
            return carry

        lax.fori_loop(0, (last - first) // size, one, 0)

    def send_terms(step, m):
        at = pl.ds(m * slab, slab)
        for k in (2, 1, 3):
            q = near_x(k)
            remote(
                terms.at[step, q, at], terms_in.at[step, col, at],
                terms_send.at[step, m], terms_recv.at[step, m], row, q,
            ).start()

    def arrive(i, carry):
        o = partner(i)
        remote(
            answers.at[i], received.at[o], answer_send, answer_recv.at[o], o, col
        ).wait_recv()
        tail32[pl.ds(pl.multiple_of(o * cap, cap), cap), :] = received[o].astype(f32)
        return carry

    lax.fori_loop(0, cuts[2], arrive, 0)

    drain(hub_z.at[pl.ds(0, planes - 1)], hub_recv.at[2])
    total = hub_ysum[...]
    for k in range(1, planes):
        total = total + hub_z[near_z(k)]
    core = lax.rem(yc, 2)
    my_piece = hub_share.at[lax.div(yc, pieces), lax.div(lax.rem(yc, pieces), 2)]
    my_piece[...] = total
    for k in range(2, ring, 2):
        remote(
            my_piece, my_piece, hub_send.at[3], hub_recv.at[3], z * ring + near_y(k), col
        ).start()
    lax.fori_loop(cuts[2], others, arrive, 0)
    tail32[pl.ds(pl.multiple_of(row * cap, cap), cap), :] = received[row].astype(f32)

    def tail_tile(l, carry):
        for i in range(tile):
            tile32[i : i + 1, :] = tail32[pl.ds(pick_s[l * tile + i], 1), :]
        factors[l + hub_tiles] = tile32[...].astype(bf16)
        return carry

    local[2].wait()

    drain(hub_y.at[pl.ds(0, ring // 2 - 1)], hub_recv.at[3])
    halves = pieces // 2
    for h in range(per_col):
        at = col * per_col + h
        for k in (2, 1, 3):
            remote(
                hub_share.at[h], hub_all.at[at, core],
                hub_send.at[4], hub_recv.at[4], row, near_x(k),
            ).start()
        hub_all[at, core] = hub_share[h]

    drain(gram_z.at[pl.ds(0, planes - 1)], gram_recv.at[2])
    gsum = gram_xsum[...]
    for k in range(1, planes):
        gsum = gsum + gram_z[near_z(k)]
    gram_all[yc] = gsum
    for k in range(1, ring):
        remote(
            gram_all.at[yc], gram_all.at[yc], gram_send.at[3], gram_recv.at[3],
            z * ring + near_y(k), col,
        ).start()
    middle = tail_tiles * 3 // 4
    lax.fori_loop(0, middle, tail_tile, 0)

    drain(hub_x.at[pl.ds(0, n_cols - 1), pl.ds(0, per_col * halves)], hub_recv.at[4])
    sibling = row + 1 - 2 * core
    for h in range(hubs):
        remote(
            hub_all.at[h, core], hub_all.at[h, core],
            hub_send.at[5], hub_recv.at[5], sibling, col,
        ).start()
    lax.fori_loop(middle, tail_tiles, tail_tile, 0)
    groups(0, start_half, 0, hub_tiles, tiles, FIRST)
    drain(hub_mine.at[pl.ds(0, n_cols // 2)], hub_recv.at[5])
    for n in range(hub_tiles):
        part = hub_all[hub_pick_s[n]]
        for m in range(halves):
            for c in range(2):
                at = (2 * m + c) * part.shape[2]
                factors[n, at : at + part.shape[2]] = part[c, m]
    groups(0, start_half, 0, 0, hub_tiles, hub_tiles)
    send_terms(0, 0)
    groups(0, start_half, 1, 0, tiles, LATER)
    send_terms(0, 1)

    def reduce_terms(step):
        for m in range(2):
            drain(
                terms_in.at[step, pl.ds(0, n_cols - 1), pl.ds(0, slab)], terms_recv.at[step, m]
            )
        total = terms[step, col]
        for k in range(1, n_cols):
            total = total + terms_in[step, near_x(k)]
        return total

    drain(gram_all.at[pl.ds(0, ring - 1)], gram_recv.at[3])
    gram_matrix = gram_all[...].reshape(gram.shape)

    def operator_rest(vector):
        return (
            jnp.dot(vector, gram_matrix, precision=highest, preferred_element_type=f32)
            + ridge * vector
        )

    solution = start[pl.ds(pl.multiple_of(col * quarter, quarter), quarter), :]
    residual = reduce_terms(0) - operator_rest(solution)
    direction = residual
    norm_now = jnp.sum(residual * residual, axis=1, keepdims=True)
    for iteration in range(ITERS):
        mine = direction_half.at[
            iteration, lax.div(col, block_quarters), lax.rem(col, block_quarters)
        ]
        mine[...] = direction.astype(bf16)
        for k in (2, 1, 3):
            remote(
                mine, mine, dir_send.at[iteration], dir_recv.at[iteration], row, near_x(k)
            ).start()
        rest = operator_rest(direction)
        drain(hub_xsum.at[pl.ds(0, dir_words)], dir_recv.at[iteration])

        for m in range(2):
            groups(iteration + 1, direction_half.at[iteration], m, 0, tiles, LATER)
            send_terms(iteration + 1, m)
        applied = reduce_terms(iteration + 1) + rest
        step_size = norm_now / (jnp.sum(direction * applied, axis=1, keepdims=True) + tiny)
        solution = solution + step_size * direction
        residual = residual - step_size * applied
        norm_next = jnp.sum(residual * residual, axis=1, keepdims=True)
        direction = residual + norm_next / (norm_now + tiny) * direction
        norm_now = norm_next
    out_ref[0] = solution
    out_ref[1] = residual

    drain(asked_out.at[pl.ds(0, n_rows - 1)], asked_sem.at[0])
    drain(answers.at[pl.ds(0, n_rows - 1)], answer_send)
    drain(hub_x.at[pl.ds(0, n_cols - 1)], hub_send.at[0])
    drain(hub_y.at[pl.ds(0, ring - 1)], hub_send.at[1])
    drain(hub_z.at[pl.ds(0, planes - 1)], hub_send.at[2])
    drain(hub_y.at[pl.ds(0, ring // 2 - 1)], hub_send.at[3])
    drain(hub_x.at[pl.ds(0, n_cols - 1), pl.ds(0, per_col * halves)], hub_send.at[4])
    drain(hub_mine.at[pl.ds(0, n_cols // 2)], hub_send.at[5])
    drain(gram_y.at[pl.ds(0, ring - 1)], gram_send.at[0])
    drain(gram_x.at[pl.ds(0, n_cols - 1)], gram_send.at[1])
    drain(gram_z.at[pl.ds(0, planes - 1)], gram_send.at[2])
    drain(gram_all.at[pl.ds(0, ring - 1)], gram_send.at[3])
    for step in range(ITERS + 1):
        for m in range(2):
            drain(
                terms_in.at[step, pl.ds(0, n_cols - 1), pl.ds(0, slab)], terms_send.at[step, m]
            )
    for iteration in range(ITERS):
        drain(hub_xsum.at[pl.ds(0, dir_words)], dir_send.at[iteration])


def per_device(
    n_rows,
    n_cols,
    mutant_factors,
    test_factors,
    weights,
    pattern,
    tile_block,
    hub_pick,
    hub_blocks,
    tail_req,
    tail_pick,
):
    mutant_rows, width = mutant_factors.shape
    tile = weights.shape[-1]
    tiles = weights.shape[2]
    hub_tiles = hub_pick.shape[2]
    hubs = hub_blocks.shape[0]
    cap = tail_req.shape[-1]
    full_rows = test_factors.shape[0]
    share = full_rows // n_cols
    slots = (tiles - hub_tiles) * tile
    ring = 8 if n_rows % 64 == 0 else 2
    planes = n_rows // ring
    per_col = hubs // n_cols
    piece = per_col * tile // ring
    gram_share = width // ring
    dims = (n_rows, n_cols, planes, ring, cap, tile, tiles, hub_tiles, hubs)
    vmem = pltpu.VMEM
    dma = pltpu.SemaphoreType.DMA
    scratch = [
        vmem((mutant_rows // tile, tile, width), bf16),
        vmem((mutant_rows, width), f32),
        vmem((full_rows, width), f32),
        vmem((tiles, tile, tile), bf16),
        vmem((tiles, tile, tile), jnp.int32),
        vmem((tiles, tile, tile), bf16),
        vmem((n_rows, cap), jnp.int32),
        pltpu.SMEM((slots,), jnp.int32),
        vmem((n_rows, 1, 128), jnp.int32),
        vmem((n_rows, 1, 128), jnp.int32),
        pltpu.SMEM((n_rows, 1, 128), jnp.int32),
        vmem((cap, width), f32),
        vmem((n_rows, cap, width), bf16),
        vmem((n_rows, cap, width), bf16),
        vmem((slots, width), f32),
        vmem((tile, width), f32),
        vmem((tiles, tile, width), bf16),
        vmem((n_cols, ring, piece, width), bf16),
        vmem((n_cols, ring, piece, width), bf16),
        vmem((ring, piece, width), bf16),
        vmem((ring, piece, width), bf16),
        vmem((piece, width), bf16),
        vmem((planes, piece, width), bf16),
        vmem((per_col, ring // per_col // 2, piece, width), bf16),
        vmem((hubs, 2, ring // per_col // 2, piece, width), bf16),
        vmem((ring, gram_share, width), f32),
        vmem((n_cols, gram_share, width), f32),
        vmem((gram_share, width), f32),
        vmem((ring, gram_share, width), f32),
        vmem((gram_share, width), f32),
        vmem((planes, gram_share, width), f32),
        vmem((ring, gram_share, width), f32),
        vmem((2, n_cols // 2, share, width), bf16),
        vmem((ITERS, 2, n_cols // 2, share, width), bf16),
        vmem((ITERS + 1, n_cols, share, width), f32),
        vmem((ITERS + 1, n_cols, share, width), f32),
        dma((7,)),
        dma((2,)),
        dma,
        dma((n_rows,)),
        dma((6,)),
        dma((6,)),
        dma((4,)),
        dma((4,)),
        dma((ITERS + 1, 2)),
        dma((ITERS + 1, 2)),
        dma((ITERS,)),
        dma((ITERS,)),
    ]
    anywhere = pl.BlockSpec(memory_space=pl.ANY)
    scalars = pl.BlockSpec(memory_space=pltpu.SMEM)
    both = pl.pallas_call(
        functools.partial(kernel, dims),
        out_shape=jax.ShapeDtypeStruct((2, share, width), f32),
        in_specs=[anywhere] * 6 + [scalars] * 3,
        out_specs=pl.BlockSpec(memory_space=vmem),
        scratch_shapes=scratch,
        compiler_params=pltpu.CompilerParams(
            collective_id=0, has_side_effects=True, vmem_limit_bytes=56 * 1024 * 1024
        ),
    )(
        mutant_factors.reshape(-1, tile, width),
        test_factors,
        weights.reshape(weights.shape[2:]),
        pattern.reshape(pattern.shape[2:]),
        tail_req.reshape(tail_req.shape[2:]),
        tail_pick.reshape(slots),
        tile_block.reshape(tiles),
        hub_pick.reshape(hub_tiles),
        hub_blocks,
    )
    return both[0], both[1]


def solution(mesh):
    in_specs = (
        P(("rows", "cols"), None),
        P("rows", None),
        P("rows", "cols", None, None, None),
        P("rows", "cols", None, None, None),
        P("rows", "cols", None),
        P("rows", "cols", None),
        P(),
        P("rows", "cols", None, None),
        P("rows", "cols", None),
    )
    out_specs = (P(("rows", "cols"), None), P(("rows", "cols"), None))
    return jax.shard_map(
        functools.partial(per_device, mesh.shape["rows"], mesh.shape["cols"]),
        mesh=mesh,
        in_specs=in_specs,
        out_specs=out_specs,
        check_vma=False,
    )
```
